32 devices in a mesh: groups: 2 (over x), band: 16 (over z, y, core).
Axes of the slice: x: 2, y: 2, z: 4, core: 2. Of those that a mesh axis runs over, the one named last changes fastest.
Arguments:
- records: bfloat16 [8192, 4096], P(None, ('groups', 'band')), parts along dimension 1, may hold values from -40 to 40
- source: int32 [4096], P(('groups', 'band')), parts along dimension 0, may hold values from 0 to 133, as said below
- weight: float32 [4096], P(('groups', 'band')), parts along dimension 0, may hold values from 0 to 1
- gap_mask: int32 [4096], P(('groups', 'band')), parts along dimension 0, may hold values from 0 to 1, as said below
Outputs:
- cleaned: bfloat16 [8, 1024, 4096], P(None, 'band', 'groups'), parts along dimension 2
- tiles: bfloat16 [32, 2, 2, 1024, 1024], P(('groups', 'band')), parts along dimension 0
The draws below stay inside these ranges and needn't reach their ends.
There are 2 independent parts, one for each index of `groups`. The reference program is written for one: setup_inputs(seed, part) draws one part's arguments, and reference() takes and returns one part's arrays. A program takes and returns all parts, laid end to end along the dimension named above; each array names one. Nothing has to cross between parts.
Inputs may be any that keep to these rules, and one draw needn't show every extreme that they name: `source`: for sample i of a device's 128 samples the value lies in i .. i + 6; it is i at a device's first sample and i + 6 at its last. `gap_mask`: on each device's 128 samples the zeros form one run of at most 32 samples that never covers the device's first sample; some device has a run of exactly that length.
All inputs are finite; a program needn't handle non-finite values.
Results may differ from the reference program's by a relative error of at most 0.0052.
Values may be sent and summed in bfloat16 or wider, within the bound.
A program may use at most 64 MiB of HBM per device.

```python
import math
import jax
import jax.numpy as jnp
from jax import lax

BLK = 1024
BLOCKS = 8
TS = 128
HALO = 8
FB = 64
F_LO = 16
CHANNELS = 8192
NT = 2048
NF = 128
N_BAND = 16


def draw_records(key, part):
    key = jax.random.fold_in(key, 11)
    subkeys = jax.random.split(key, 3)
    noise_values = jax.random.normal(subkeys[0], (CHANNELS, NT), jnp.float32)
    scale_low, scale_high, offset_range = (0.3, 3.0, 2.0)
    channel_scale = jnp.exp(jax.random.uniform(subkeys[1], (CHANNELS, 1), jnp.float32, math.log(scale_low), math.log(scale_high)))
    channel_offset = jax.random.uniform(subkeys[2], (CHANNELS, 1), jnp.float32, -offset_range, offset_range)
    time_trend = 1.0 + 2.0 * jnp.arange(NT, dtype=jnp.float32) / NT
    return (noise_values * channel_scale + channel_offset * time_trend[None, :]).astype(jnp.bfloat16)


def draw_source(key, part):
    key = jax.random.fold_in(key, 23)
    position = jnp.arange(NT, dtype=jnp.int32) % TS
    sample_lag = jax.random.randint(key, (NT,), 0, HALO - 1, dtype=jnp.int32)
    sample_lag = jnp.where(position == 0, 0, jnp.where(position == TS - 1, HALO - 2, sample_lag))
    return (position + sample_lag).astype(jnp.int32)


def draw_gap_mask(key, part):
    key = jax.random.fold_in(key, 37)
    start_key, length_key = jax.random.split(key)
    shards = NT // TS
    longest = TS // 4
    gap_start = jax.random.randint(start_key, (shards,), 1, TS - longest + 1, dtype=jnp.int32)
    gap_length = jax.random.randint(length_key, (shards,), 0, longest + 1, dtype=jnp.int32)
    gap_length = jnp.where(jnp.arange(shards, dtype=jnp.int32) == 0, longest, gap_length)
    position = jnp.arange(NT, dtype=jnp.int32) % TS
    shard_index = jnp.arange(NT, dtype=jnp.int32) // TS
    begins = gap_start[shard_index]
    inside = (position >= begins) & (position < begins + gap_length[shard_index])
    return jnp.where(inside, 0, 1).astype(jnp.int32)


def levels(stream_key, extent, pieces, low, top_value):
    loudness, own = 1.0, jax.random.fold_in(stream_key, 6)
    for dim, parts in pieces:
        steps = jnp.exp(jax.random.uniform(jax.random.fold_in(own, dim), (parts,), jnp.float32, low / len(pieces), top_value / len(pieces)))
        loudness = loudness * jnp.repeat(steps, extent[dim] // parts).reshape([-1 if axis == dim else 1 for axis in range(len(extent))])
    return loudness


def setup_inputs(seed: int = 0, part: int = 0) -> dict:
    keys = jax.random.split(jax.random.key(seed), 5)
    part_keys = jax.random.split(jax.random.fold_in(keys[4], part), 5)
    records = draw_records(jax.random.fold_in(jax.random.fold_in(keys[4], part), 71), part)
    source = draw_source(jax.random.fold_in(jax.random.fold_in(keys[4], part), 71), part)
    weight = jnp.clip(1.0 * jax.random.uniform(part_keys[2], (NT,), jnp.float32) ** levels(part_keys[2], (NT,), ((0, 16),), -0.2, 0.2), 0.0, 1.0)
    gap_mask = draw_gap_mask(jax.random.fold_in(jax.random.fold_in(keys[4], part), 71), part)
    return {"records": records, "source": source, "weight": weight, "gap_mask": gap_mask}


epsilon = 1e-06

def harmonic_matrix(acquisition_moments, spectral_line_total, trace_duration):
    cycles_per_second = F_LO + jnp.arange(spectral_line_total, dtype=jnp.int32)
    angle_step = acquisition_moments[:, None] * cycles_per_second[None, :] % trace_duration
    phase_angle = angle_step.astype(jnp.float32) * (2.0 * math.pi / trace_duration)
    return jnp.concatenate([jnp.cos(phase_angle), -jnp.sin(phase_angle)], axis=1).astype(jnp.bfloat16)

def interpolate(padded, sample_index, weight, gap_mask):
    lower_value = jnp.take(padded, sample_index, axis=1).astype(jnp.float32)
    higher_value = jnp.take(padded, sample_index + 1, axis=1).astype(jnp.float32)
    return gap_mask.astype(jnp.float32) * ((1.0 - weight) * lower_value + weight * higher_value)

def whiten(spectra):
    values = spectra.astype(jnp.float32)
    band_power = lax.optimization_barrier(jnp.sum(values * values, axis=(-3, -2))) / values.shape[-2]
    return (values * lax.rsqrt(band_power + epsilon)[..., None, None, :]).astype(jnp.bfloat16)

def pair_tiles(own_block, following):
    stacked_bins = own_block.shape[0] * own_block.shape[1]
    left_side = own_block.reshape(stacked_bins, -1).astype(jnp.float32)

    def columns(spectra):
        return jnp.stack([spectra.reshape(stacked_bins, -1), jnp.concatenate([spectra[1], -spectra[0]], axis=0)])
    right_side = jnp.concatenate([columns(own_block), columns(following)], axis=0).astype(jnp.float32)
    pair_tile = jnp.einsum('fi,pfj->pij', left_side, right_side)
    width_out = left_side.shape[1]
    return (pair_tile / own_block.shape[1]).astype(jnp.bfloat16).reshape(2, 2, width_out, width_out)

def reference(records, source, weight, gap_mask):
    channels, taper_span = records.shape
    sample_index = source + jnp.arange(taper_span, dtype=jnp.int32) // TS * TS
    kernel_table = harmonic_matrix(jnp.arange(taper_span, dtype=jnp.int32), NF, taper_span).astype(jnp.float32)
    blocked = records.reshape(BLOCKS, BLK, taper_span)
    mask_float = gap_mask.astype(jnp.float32)
    valid_count = jnp.sum(mask_float)

    def condition(spectra_rows):
        padded = jnp.concatenate([spectra_rows, jnp.zeros((BLK, HALO), spectra_rows.dtype)], axis=1)
        resampled = interpolate(padded, sample_index, weight, gap_mask)
        centre = lax.optimization_barrier(jnp.sum(resampled, axis=1)) / valid_count
        cleaned_rows = (mask_float * (resampled - centre[:, None])).astype(jnp.bfloat16)
        spectrum = jnp.dot(cleaned_rows.astype(jnp.float32), kernel_table, precision=lax.Precision.HIGHEST).astype(jnp.bfloat16)
        return (cleaned_rows, spectrum)
    cleaned, spectrum = lax.map(condition, blocked)
    band_count = N_BAND // BLOCKS
    band_parts = spectrum.reshape(BLOCKS, BLK, 2, band_count, FB).transpose(3, 0, 2, 4, 1)
    whitened = whiten(band_parts)
    following = jnp.concatenate([whitened[:, 1:], jnp.zeros_like(whitened[:, :1])], axis=1)
    own_flat = whitened.reshape(band_count * BLOCKS, 2, FB, BLK)
    next_flat = following.reshape(band_count * BLOCKS, 2, FB, BLK)
    tiles = lax.map(lambda couple: pair_tiles(couple[0], couple[1]), (own_flat, next_flat))
    return (cleaned, tiles)
```

```python
import functools
import math

import jax
import jax.numpy as jnp
from jax import lax
from jax.experimental import pallas as pl
from jax.experimental.pallas import tpu as pltpu
from jax.sharding import PartitionSpec as P

BLOCKS = 8
HALO = 8
FB = 64
F_LO = 16


epsilon = 1e-06


def passed_along(block, axis, distance):
    devices = range(lax.axis_size(axis))
    route = [(i - distance, i) for i in devices if i - distance in devices]
    return lax.ppermute(block, axis, route)


def harmonic_matrix(acquisition_moments, spectral_line_total, trace_duration):
    cycles_per_second = F_LO + jnp.arange(spectral_line_total, dtype=jnp.int32)
    angle_step = acquisition_moments[:, None] * cycles_per_second[None, :] % trace_duration
    phase_angle = angle_step.astype(jnp.float32) * (2.0 * math.pi / trace_duration)
    return jnp.concatenate([jnp.cos(phase_angle), -jnp.sin(phase_angle)], axis=1).astype(
        jnp.bfloat16
    )


def spread_matrix(source, weight, gap_mask, span):
    positions = jnp.arange(span, dtype=jnp.int32)[:, None]
    lower_hit = (positions == source[..., None, :]).astype(jnp.float32)
    upper_hit = (positions == source[..., None, :] + 1).astype(jnp.float32)
    mask_float = gap_mask.astype(jnp.float32)[..., None, :]
    return mask_float * (
        (1.0 - weight[..., None, :]) * lower_hit + weight[..., None, :] * upper_hit
    )


def whiten(spectra):
    values = spectra.astype(jnp.float32)
    band_power = jnp.sum(values * values, axis=(-3, -2)) / values.shape[-2]
    return (values * lax.rsqrt(band_power + epsilon)[..., None, None, :]).astype(jnp.bfloat16)


def pair_tiles(own_block, following):
    stacked_bins = own_block.shape[0] * own_block.shape[1]
    left_side = own_block.reshape(stacked_bins, -1).astype(jnp.float32)

    def columns(spectra):
        return jnp.stack(
            [spectra.reshape(stacked_bins, -1), jnp.concatenate([spectra[1], -spectra[0]], axis=0)]
        )

    right_side = jnp.concatenate([columns(own_block), columns(following)], axis=0).astype(
        jnp.float32
    )
    pair_tile = jnp.einsum("fi,pfj->pij", left_side, right_side, precision=lax.Precision.HIGHEST)
    width_out = left_side.shape[1]
    return (pair_tile / own_block.shape[1]).astype(jnp.bfloat16).reshape(2, 2, width_out, width_out)


def per_device_collectives(records, source, weight, gap_mask):
    devices = lax.axis_size("band")
    channels, shard_len = records.shape
    block_width = channels // BLOCKS
    mask_float = gap_mask.astype(jnp.float32)
    carried = passed_along(records[:, :HALO], "band", -1)
    padded = jnp.concatenate([records, carried], axis=1).astype(jnp.float32)
    spreader = spread_matrix(source, weight, gap_mask, shard_len + HALO)
    resampled = jnp.dot(padded, spreader, precision=lax.Precision.HIGHEST)
    totals, valid_count = lax.psum((jnp.sum(resampled, axis=1), jnp.sum(mask_float)), "band")
    local_clean = (mask_float * (resampled - (totals / valid_count)[:, None])).astype(jnp.bfloat16)
    cleaned = lax.all_to_all(
        local_clean.reshape(BLOCKS, block_width, shard_len),
        "band",
        split_axis=1,
        concat_axis=2,
        tiled=True,
    )
    taper_span = cleaned.shape[2]
    stripe_rows = cleaned.reshape(-1, taper_span)
    band_count = devices // BLOCKS
    spectral_line_total = FB * band_count
    segment_span = min(1024, taper_span)

    def accumulate(block_step, running):
        first_moment = block_step * segment_span
        window_rows = lax.dynamic_slice_in_dim(stripe_rows, first_moment, segment_span, 1).astype(
            jnp.float32
        )
        acquisition_moments = first_moment + jnp.arange(segment_span, dtype=jnp.int32)
        kernel_part = harmonic_matrix(acquisition_moments, spectral_line_total, taper_span).astype(
            jnp.float32
        )
        return running + jnp.dot(window_rows, kernel_part, precision=lax.Precision.HIGHEST)

    spectrum = lax.fori_loop(
        0,
        taper_span // segment_span,
        accumulate,
        jnp.zeros((stripe_rows.shape[0], 2 * spectral_line_total), jnp.float32),
    )
    spectrum = spectrum.astype(jnp.bfloat16)
    band_parts = spectrum.reshape(BLOCKS, -1, 2, band_count, FB).transpose(3, 0, 2, 4, 1)
    stripe_width = band_parts.shape[4]
    arrived = lax.all_to_all(
        band_parts.reshape(devices, 2, FB, stripe_width),
        "band",
        split_axis=0,
        concat_axis=3,
        tiled=True,
    )
    own_block = whiten(arrived[0])
    neighbour = passed_along(own_block, "band", -1)
    position = lax.axis_index("band") % BLOCKS
    following = jnp.where(position == BLOCKS - 1, jnp.zeros_like(neighbour), neighbour)
    return (cleaned, pair_tiles(own_block, following)[None])


LOOKAHEAD = 3
MESH = pl.DeviceIdType.MESH


def half_turn_cosine(steps, turn):
    folded = jnp.minimum(steps, turn - steps).astype(jnp.float32)
    y = (0.25 * turn - folded) * (2.0 * math.pi / turn)
    y2 = y * y
    total = jnp.full_like(y, -1.0 / 39916800.0)
    for term in (1.0 / 362880.0, -1.0 / 5040.0, 1.0 / 120.0, -1.0 / 6.0, 1.0):
        total = total * y2 + term
    return total * y


def exchange_kernel(
    n,
    records,
    source,
    weight,
    gap_mask,
    cleaned,
    own_out,
    next_out,
    info,
    infos,
    raw,
    resampled,
    clean,
    table,
    spectra,
    own,
    following,
    info_send,
    info_recv,
    raw_send,
    raw_recv,
    raw_local,
    clean_sem,
    spec_send,
    spec_recv,
    pass_send,
    pass_recv,
):
    me = lax.axis_index("band")
    shard_len = records.shape[1]
    block_width = records.shape[0] // BLOCKS
    stripe = block_width // n
    bands = n // BLOCKS
    span = n * shard_len
    my_block = lax.rem(me, BLOCKS)

    barrier = pltpu.get_barrier_semaphore()

    def greet(j, carry):
        pl.semaphore_signal(
            barrier, inc=1, device_id={"band": lax.rem(me + j, n)}, device_id_type=MESH
        )
        return carry

    lax.fori_loop(1, n, greet, 0)

    row = lax.broadcasted_iota(jnp.int32, (HALO, shard_len), 0)
    lane = lax.broadcasted_iota(jnp.int32, (HALO, shard_len), 1)
    offset = source[...] - lane
    mask_row = gap_mask[...].astype(jnp.float32)
    upper = weight[...]
    info[:HALO] = mask_row * (
        jnp.where(offset == row, 1.0 - upper, 0.0) + jnp.where(offset + 1 == row, upper, 0.0)
    )
    info[HALO:] = jnp.broadcast_to(mask_row, (HALO, shard_len))
    infos[me] = info[...]

    def local_copy(k):
        start = pl.multiple_of(k * block_width + me * stripe, stripe)
        return pltpu.make_async_copy(
            records.at[pl.ds(start, stripe)], raw.at[k, me], raw_local.at[k]
        )

    def start_local(k, carry):
        local_copy(k).start()
        return carry

    lax.fori_loop(0, BLOCKS, start_local, 0)
    pl.semaphore_wait(barrier, n - 1)

    def send_info(j, carry):
        pltpu.make_async_remote_copy(
            src_ref=info,
            dst_ref=infos.at[me],
            send_sem=info_send,
            recv_sem=info_recv,
            device_id={"band": lax.rem(me + j, n)},
            device_id_type=MESH,
        ).start()
        return carry

    lax.fori_loop(1, n, send_info, 0)

    def send_block(k):
        def send(j, carry):
            to = lax.rem(me + j, n)
            start = pl.multiple_of(k * block_width + to * stripe, stripe)
            pltpu.make_async_remote_copy(
                src_ref=records.at[pl.ds(start, stripe)],
                dst_ref=raw.at[k, me],
                send_sem=raw_send,
                recv_sem=raw_recv.at[k],
                device_id={"band": to},
                device_id_type=MESH,
            ).start()
            return carry

        lax.fori_loop(1, n, send, 0)

    for k in range(BLOCKS - 1, BLOCKS - 1 - LOOKAHEAD, -1):
        send_block(k)

    for k in range(BLOCKS):
        raw[k, n] = jnp.zeros((stripe, shard_len), raw.dtype)

    moments = 128

    def fill(step, carry):
        shape = (moments, 2 * FB)
        t = step * moments + lax.broadcasted_iota(jnp.int32, shape, 0)
        column = lax.broadcasted_iota(jnp.int32, shape, 1)
        part = column // FB
        for q in range(bands):
            f = F_LO + q * FB + column - part * FB
            steps = (t * f + part * (span // 4)) & (span - 1)
            start = pl.multiple_of(step * moments, moments)
            table[pl.ds(start, moments), q * 2 * FB : (q + 1) * 2 * FB] = half_turn_cosine(
                steps, span
            ).astype(table.dtype)
        return carry

    lax.fori_loop(0, span // moments, fill, 0)

    others = pl.ds(0, n - 1)
    pltpu.make_async_copy(infos.at[others], infos.at[others], info_recv).wait()
    count = jnp.sum(infos[:, HALO, :])

    lane = lax.broadcasted_iota(jnp.int32, (stripe, shard_len), 1)

    def one_block(i, carry):
        k = BLOCKS - 1 - i

        @pl.when(k >= LOOKAHEAD)
        def _():
            send_block(k - LOOKAHEAD)

        pltpu.make_async_copy(raw.at[k, others], raw.at[k, others], raw_recv.at[k]).wait()
        local_copy(k).wait()

        def resample(s, total):
            here = raw[k, s].astype(jnp.float32)
            after = raw[k, s + 1].astype(jnp.float32)
            value = here * infos[s, 0:1, :]
            for d in range(1, HALO):
                shifted = pltpu.roll(jnp.where(lane >= d, here, after), shard_len - d, 1)
                value = value + shifted * infos[s, d : d + 1, :]
            resampled[s] = value
            return total + value

        total = lax.fori_loop(0, n, resample, jnp.zeros((stripe, shard_len), jnp.float32))
        centre = jnp.sum(total, axis=1, keepdims=True) / count
        for s in range(n):
            clean[k, :, s * shard_len : (s + 1) * shard_len] = (
                infos[s, HALO : HALO + 1, :] * (resampled[s] - centre)
            ).astype(clean.dtype)
        pltpu.make_async_copy(clean.at[k], cleaned.at[k], clean_sem.at[k]).start()
        result = jnp.dot(clean[k], table[...], preferred_element_type=jnp.float32)
        for q in range(bands):
            spectra[k, q] = result[:, q * 2 * FB : (q + 1) * 2 * FB].astype(spectra.dtype)
            to = q * BLOCKS + k

            @pl.when(to == me)
            def _():
                own[me] = spectra[k, q]

            @pl.when(to != me)
            def _():
                pltpu.make_async_remote_copy(
                    src_ref=spectra.at[k, q],
                    dst_ref=own.at[me],
                    send_sem=spec_send,
                    recv_sem=spec_recv,
                    device_id={"band": to},
                    device_id_type=MESH,
                ).start()

        @pl.when(my_block == k + 1)
        def _():
            wait_own()
            pass_on().start()

        return carry

    def wait_own():
        pltpu.make_async_copy(own.at[others], own.at[others], spec_recv).wait()

    def pass_on():
        return pltpu.make_async_remote_copy(
            src_ref=own,
            dst_ref=following,
            send_sem=pass_send,
            recv_sem=pass_recv,
            device_id={"band": lax.rem(me + n - 1, n)},
            device_id_type=MESH,
        )

    lax.fori_loop(0, BLOCKS, one_block, 0)

    @pl.when(my_block == 0)
    def _():
        wait_own()

    @pl.when(my_block != 0)
    def _():
        pass_on().wait_send()

    @pl.when(my_block == BLOCKS - 1)
    def _():
        following[...] = jnp.zeros_like(following)

    @pl.when(my_block != BLOCKS - 1)
    def _():
        pltpu.make_async_copy(following, following, pass_recv).wait()

    own_out[...] = own[...]
    next_out[...] = following[...]

    def finish(k, carry):
        pltpu.make_async_copy(clean.at[k], cleaned.at[k], clean_sem.at[k]).wait()
        return carry

    lax.fori_loop(0, BLOCKS, finish, 0)
    sent = records.at[pl.ds(0, (n - 1) * BLOCKS * stripe)]
    pltpu.make_async_copy(sent, sent, raw_send).wait()
    pltpu.make_async_copy(infos.at[others], infos.at[others], info_send).wait()
    pltpu.make_async_copy(own.at[others], own.at[others], spec_send).wait()


def exchange(records, source, weight, gap_mask, n):
    channels, shard_len = records.shape
    stripe = channels // BLOCKS // n
    bands = n // BLOCKS
    span = n * shard_len
    vmem = pl.BlockSpec(memory_space=pltpu.VMEM)
    hbm = pl.BlockSpec(memory_space=pl.ANY)
    gathered = jax.ShapeDtypeStruct((n, stripe, 2 * FB), jnp.bfloat16)
    dma = pltpu.SemaphoreType.DMA
    return pl.pallas_call(
        functools.partial(exchange_kernel, n),
        out_shape=(
            jax.ShapeDtypeStruct((BLOCKS, stripe, span), jnp.bfloat16),
            gathered,
            gathered,
        ),
        in_specs=[hbm, vmem, vmem, vmem],
        out_specs=(hbm, vmem, vmem),
        scratch_shapes=[
            pltpu.VMEM((2 * HALO, shard_len), jnp.float32),
            pltpu.VMEM((n, 2 * HALO, shard_len), jnp.float32),
            pltpu.VMEM((BLOCKS, n + 1, stripe, shard_len), jnp.bfloat16),
            pltpu.VMEM((n, stripe, shard_len), jnp.float32),
            pltpu.VMEM((BLOCKS, stripe, span), jnp.bfloat16),
            pltpu.VMEM((span, 2 * FB * bands), jnp.bfloat16),
            pltpu.VMEM((BLOCKS, bands, stripe, 2 * FB), jnp.bfloat16),
            pltpu.VMEM((n, stripe, 2 * FB), jnp.bfloat16),
            pltpu.VMEM((n, stripe, 2 * FB), jnp.bfloat16),
            dma,
            dma,
            dma,
            dma((BLOCKS,)),
            dma((BLOCKS,)),
            dma((BLOCKS,)),
            dma,
            dma,
            dma,
            dma,
        ],
        compiler_params=pltpu.CompilerParams(
            collective_id=0, has_side_effects=True, vmem_limit_bytes=40 * 2**20
        ),
        name="exchange",
    )(records, source.reshape(1, -1), weight.reshape(1, -1), gap_mask.reshape(1, -1))


def tiles_kernel(own, following, cleaned, tiles, cleaned_out, left, right, sem):
    pair, part, rows = pl.program_id(0), pl.program_id(1), pl.program_id(2)
    first = (pair == 0) & (part == 0) & (rows == 0)
    last = (pair == 1) & (part == 1) & (rows == pl.num_programs(2) - 1)

    @pl.when(first)
    def _():
        pltpu.make_async_copy(cleaned, cleaned_out, sem).start()
        negate = lax.broadcasted_iota(jnp.int32, own.shape, 1) >= FB
        for p, block in enumerate((own, following)):
            values = block[...].astype(jnp.float32)
            band_power = jnp.sum(values * values, axis=1, keepdims=True) / FB
            white = (values * lax.rsqrt(band_power + epsilon)).astype(jnp.bfloat16)
            if p == 0:
                left[...] = white
            right[2 * p] = white
            turned = pltpu.roll(white.astype(jnp.float32), FB, 1)
            right[2 * p + 1] = jnp.where(negate, -turned, turned).astype(jnp.bfloat16)

    height = tiles.shape[3]
    start = pl.multiple_of(rows * height, height)
    product = lax.dot_general(
        left[pl.ds(start, height), :],
        right[2 * pair + part],
        (((1,), (1,)), ((), ())),
        preferred_element_type=jnp.float32,
    )
    tiles[0, 0, 0] = (product * (1.0 / FB)).astype(tiles.dtype)

    @pl.when(last)
    def _():
        pltpu.make_async_copy(cleaned, cleaned_out, sem).wait()


def make_tiles(own, following, cleaned):
    width = own.shape[0]
    height = min(512, width)
    vmem = pl.BlockSpec(memory_space=pltpu.VMEM)
    hbm = pl.BlockSpec(memory_space=pl.ANY)
    return pl.pallas_call(
        tiles_kernel,
        grid=(2, 2, width // height),
        out_shape=(
            jax.ShapeDtypeStruct((1, 2, 2, width, width), jnp.bfloat16),
            jax.ShapeDtypeStruct(cleaned.shape, cleaned.dtype),
        ),
        in_specs=[vmem, vmem, hbm],
        out_specs=(
            pl.BlockSpec((1, 1, 1, height, width), lambda p, c, r: (0, p, c, r, 0)),
            hbm,
        ),
        scratch_shapes=[
            pltpu.VMEM((width, 2 * FB), jnp.bfloat16),
            pltpu.VMEM((4, width, 2 * FB), jnp.bfloat16),
            pltpu.SemaphoreType.DMA,
        ],
        compiler_params=pltpu.CompilerParams(vmem_limit_bytes=32 * 2**20),
        name="tiles",
    )(own, following, cleaned)


def per_device(records, source, weight, gap_mask):
    n = lax.axis_size("band")
    channels, shard_len = records.shape
    stripe = channels // BLOCKS // n
    span = n * shard_len
    if stripe % 16 or shard_len != 128 or span & (span - 1) or span > 4096:
        return per_device_collectives(records, source, weight, gap_mask)
    cleaned, own, following = exchange(records, source, weight, gap_mask, n)
    width = n * stripe
    tiles, cleaned = make_tiles(own.reshape(width, -1), following.reshape(width, -1), cleaned)
    return cleaned, tiles


def solution(mesh):
    placed = (
        P(None, ("groups", "band")),
        P(("groups", "band")),
        P(("groups", "band")),
        P(("groups", "band")),
    )
    return jax.shard_map(
        per_device,
        mesh=mesh,
        in_specs=placed,
        out_specs=(P(None, "band", "groups"), P(("groups", "band"), None, None, None, None)),
        check_vma=False,
    )
```

```python
import functools
import math

import jax
import jax.numpy as jnp
from jax import lax
from jax.experimental import pallas as pl
from jax.experimental.pallas import tpu as pltpu
from jax.sharding import PartitionSpec as P

BLOCKS = 8
HALO = 8
FB = 64
F_LO = 16


epsilon = 1e-06


def passed_along(block, axis, distance):
    devices = range(lax.axis_size(axis))
    route = [(i - distance, i) for i in devices if i - distance in devices]
    return lax.ppermute(block, axis, route)


def harmonic_matrix(acquisition_moments, spectral_line_total, trace_duration):
    cycles_per_second = F_LO + jnp.arange(spectral_line_total, dtype=jnp.int32)
    angle_step = acquisition_moments[:, None] * cycles_per_second[None, :] % trace_duration
    phase_angle = angle_step.astype(jnp.float32) * (2.0 * math.pi / trace_duration)
    return jnp.concatenate([jnp.cos(phase_angle), -jnp.sin(phase_angle)], axis=1).astype(
        jnp.bfloat16
    )


def spread_matrix(source, weight, gap_mask, span):
    positions = jnp.arange(span, dtype=jnp.int32)[:, None]
    lower_hit = (positions == source[..., None, :]).astype(jnp.float32)
    upper_hit = (positions == source[..., None, :] + 1).astype(jnp.float32)
    mask_float = gap_mask.astype(jnp.float32)[..., None, :]
    return mask_float * (
        (1.0 - weight[..., None, :]) * lower_hit + weight[..., None, :] * upper_hit
    )


def whiten(spectra):
    values = spectra.astype(jnp.float32)
    band_power = jnp.sum(values * values, axis=(-3, -2)) / values.shape[-2]
    return (values * lax.rsqrt(band_power + epsilon)[..., None, None, :]).astype(jnp.bfloat16)


def pair_tiles(own_block, following):
    stacked_bins = own_block.shape[0] * own_block.shape[1]
    left_side = own_block.reshape(stacked_bins, -1).astype(jnp.float32)

    def columns(spectra):
        return jnp.stack(
            [spectra.reshape(stacked_bins, -1), jnp.concatenate([spectra[1], -spectra[0]], axis=0)]
        )

    right_side = jnp.concatenate([columns(own_block), columns(following)], axis=0).astype(
        jnp.float32
    )
    pair_tile = jnp.einsum("fi,pfj->pij", left_side, right_side, precision=lax.Precision.HIGHEST)
    width_out = left_side.shape[1]
    return (pair_tile / own_block.shape[1]).astype(jnp.bfloat16).reshape(2, 2, width_out, width_out)


def per_device_collectives(records, source, weight, gap_mask):
    devices = lax.axis_size("band")
    channels, shard_len = records.shape
    block_width = channels // BLOCKS
    mask_float = gap_mask.astype(jnp.float32)
    carried = passed_along(records[:, :HALO], "band", -1)
    padded = jnp.concatenate([records, carried], axis=1).astype(jnp.float32)
    spreader = spread_matrix(source, weight, gap_mask, shard_len + HALO)
    resampled = jnp.dot(padded, spreader, precision=lax.Precision.HIGHEST)
    totals, valid_count = lax.psum((jnp.sum(resampled, axis=1), jnp.sum(mask_float)), "band")
    local_clean = (mask_float * (resampled - (totals / valid_count)[:, None])).astype(jnp.bfloat16)
    cleaned = lax.all_to_all(
        local_clean.reshape(BLOCKS, block_width, shard_len),
        "band",
        split_axis=1,
        concat_axis=2,
        tiled=True,
    )
    taper_span = cleaned.shape[2]
    stripe_rows = cleaned.reshape(-1, taper_span)
    band_count = devices // BLOCKS
    spectral_line_total = FB * band_count
    segment_span = min(1024, taper_span)

    def accumulate(block_step, running):
        first_moment = block_step * segment_span
        window_rows = lax.dynamic_slice_in_dim(stripe_rows, first_moment, segment_span, 1).astype(
            jnp.float32
        )
        acquisition_moments = first_moment + jnp.arange(segment_span, dtype=jnp.int32)
        kernel_part = harmonic_matrix(acquisition_moments, spectral_line_total, taper_span).astype(
            jnp.float32
        )
        return running + jnp.dot(window_rows, kernel_part, precision=lax.Precision.HIGHEST)

    spectrum = lax.fori_loop(
        0,
        taper_span // segment_span,
        accumulate,
        jnp.zeros((stripe_rows.shape[0], 2 * spectral_line_total), jnp.float32),
    )
    spectrum = spectrum.astype(jnp.bfloat16)
    band_parts = spectrum.reshape(BLOCKS, -1, 2, band_count, FB).transpose(3, 0, 2, 4, 1)
    stripe_width = band_parts.shape[4]
    arrived = lax.all_to_all(
        band_parts.reshape(devices, 2, FB, stripe_width),
        "band",
        split_axis=0,
        concat_axis=3,
        tiled=True,
    )
    own_block = whiten(arrived[0])
    neighbour = passed_along(own_block, "band", -1)
    position = lax.axis_index("band") % BLOCKS
    following = jnp.where(position == BLOCKS - 1, jnp.zeros_like(neighbour), neighbour)
    return (cleaned, pair_tiles(own_block, following)[None])


LOOKAHEAD = 3
PASS_DELAY = 2
MESH = pl.DeviceIdType.MESH


def half_turn_cosine(steps, turn):
    folded = jnp.minimum(steps, turn - steps).astype(jnp.float32)
    y = (0.25 * turn - folded) * (2.0 * math.pi / turn)
    y2 = y * y
    total = jnp.full_like(y, -1.0 / 39916800.0)
    for term in (1.0 / 362880.0, -1.0 / 5040.0, 1.0 / 120.0, -1.0 / 6.0, 1.0):
        total = total * y2 + term
    return total * y


def exchange_kernel(
    n,
    records_in,
    source_in,
    weight_in,
    gap_mask_in,
    cleaned,
    own_out,
    next_out,
    records,
    source,
    weight,
    gap_mask,
    small_sem,
    fetch_sem,
    info,
    infos,
    raw,
    resampled,
    clean,
    table,
    spectra,
    own,
    following,
    info_send,
    info_recv,
    raw_send,
    raw_recv,
    raw_local,
    clean_sem,
    spec_send,
    spec_recv,
    pass_send,
    pass_recv,
    out_sem,
):
    me = lax.axis_index("band")
    shard_len = records.shape[1]
    block_width = records.shape[0] // BLOCKS
    stripe = block_width // n
    bands = n // BLOCKS
    span = n * shard_len
    my_block = lax.rem(me, BLOCKS)

    barrier = pltpu.get_barrier_semaphore()

    def greet(j, carry):
        pl.semaphore_signal(
            barrier, inc=1, device_id={"band": lax.rem(me + j, n)}, device_id_type=MESH
        )
        return carry

    lax.fori_loop(1, n, greet, 0)

    small = [
        pltpu.make_async_copy(there, here, small_sem.at[a])
        for a, (there, here) in enumerate(
            ((source_in, source), (weight_in, weight), (gap_mask_in, gap_mask))
        )
    ]
    for copy in small:
        copy.start()

    def fetch(k):
        rows = pl.ds(pl.multiple_of(k * block_width, block_width), block_width)
        return pltpu.make_async_copy(records_in.at[rows], records.at[rows], fetch_sem.at[k])

    for k in range(BLOCKS - 1, -1, -1):
        fetch(k).start()
    for copy in small:
        copy.wait()

    row = lax.broadcasted_iota(jnp.int32, (HALO, shard_len), 0)
    lane = lax.broadcasted_iota(jnp.int32, (HALO, shard_len), 1)
    offset = source[...] - lane
    mask_row = gap_mask[...].astype(jnp.float32)
    upper = weight[...]
    info[:HALO] = mask_row * (
        jnp.where(offset == row, 1.0 - upper, 0.0) + jnp.where(offset + 1 == row, upper, 0.0)
    )
    info[HALO:] = jnp.broadcast_to(mask_row, (HALO, shard_len))
    infos[me] = info[...]

    def local_copy(k):
        start = pl.multiple_of(k * block_width + me * stripe, stripe)
        return pltpu.make_async_copy(
            records.at[pl.ds(start, stripe)], raw.at[k, me], raw_local.at[k]
        )

    pl.semaphore_wait(barrier, n - 1)

    def send_info(j, carry):
        pltpu.make_async_remote_copy(
            src_ref=info,
            dst_ref=infos.at[me],
            send_sem=info_send,
            recv_sem=info_recv,
            device_id={"band": lax.rem(me + j, n)},
            device_id_type=MESH,
        ).start()
        return carry


    def send_block(k):
        fetch(k).wait()
        local_copy(k).start()

        def send(j, carry):
            turn = (j % 2) * (n // 2) + j // 2
            to, bit = 0, 1
            while bit < n:
                to = to + bit * ((me // bit + turn // bit) % 2)
                bit *= 2
            start = pl.multiple_of(k * block_width + to * stripe, stripe)
            pltpu.make_async_remote_copy(
                src_ref=records.at[pl.ds(start, stripe)],
                dst_ref=raw.at[k, me],
                send_sem=raw_send,
                recv_sem=raw_recv.at[k],
                device_id={"band": to},
                device_id_type=MESH,
            ).start()
            return carry

        lax.fori_loop(1, n, send, 0)

    send_block(BLOCKS - 1)
    lax.fori_loop(1, n, send_info, 0)
    for k in range(BLOCKS - 2, BLOCKS - 1 - LOOKAHEAD, -1):
        send_block(k)

    for k in range(BLOCKS):
        raw[k, n] = jnp.zeros((stripe, shard_len), raw.dtype)

    moments = 128

    def fill(step, carry):
        shape = (moments, 2 * FB)
        t = step * moments + lax.broadcasted_iota(jnp.int32, shape, 0)
        column = lax.broadcasted_iota(jnp.int32, shape, 1)
        part = column // FB
        for q in range(bands):
            f = F_LO + q * FB + column - part * FB
            steps = (t * f + part * (span // 4)) & (span - 1)
            start = pl.multiple_of(step * moments, moments)
            table[pl.ds(start, moments), q * 2 * FB : (q + 1) * 2 * FB] = half_turn_cosine(
                steps, span
            ).astype(table.dtype)
        return carry

    lax.fori_loop(0, span // moments, fill, 0)

    others = pl.ds(0, n - 1)
    pltpu.make_async_copy(infos.at[others], infos.at[others], info_recv).wait()
    count = jnp.sum(infos[:, HALO, :])

    lane = lax.broadcasted_iota(jnp.int32, (stripe, shard_len), 1)

    def one_block(i, carry):
        k = BLOCKS - 1 - i

        @pl.when(k >= LOOKAHEAD)
        def _():
            send_block(k - LOOKAHEAD)

        pltpu.make_async_copy(raw.at[k, others], raw.at[k, others], raw_recv.at[k]).wait()
        local_copy(k).wait()

        def resample_one(s, total):
            here = raw[k, s].astype(jnp.float32)
            after = raw[k, s + 1].astype(jnp.float32)
            value = here * infos[s, 0:1, :]
            for d in range(1, HALO):
                shifted = pltpu.roll(jnp.where(lane >= d, here, after), shard_len - d, 1)
                value = value + shifted * infos[s, d : d + 1, :]
            resampled[s] = value
            return total + value

        def resample(group, total):
            for s in range(4):
                total = resample_one(4 * group + s, total)
            return total

        total = lax.fori_loop(0, n // 4, resample, jnp.zeros((stripe, shard_len), jnp.float32))
        centre = jnp.sum(total, axis=1, keepdims=True) / count
        for s in range(n):
            clean[k, :, s * shard_len : (s + 1) * shard_len] = (
                infos[s, HALO : HALO + 1, :] * (resampled[s] - centre)
            ).astype(clean.dtype)
        pltpu.make_async_copy(clean.at[k], cleaned.at[k], clean_sem.at[k]).start()
        result = jnp.dot(clean[k], table[...], preferred_element_type=jnp.float32)
        for q in range(bands):
            spectra[k, q] = result[:, q * 2 * FB : (q + 1) * 2 * FB].astype(spectra.dtype)
            to = q * BLOCKS + k

            @pl.when(to == me)
            def _():
                own[me] = spectra[k, q]

            @pl.when(to != me)
            def _():
                pltpu.make_async_remote_copy(
                    src_ref=spectra.at[k, q],
                    dst_ref=own.at[me],
                    send_sem=spec_send,
                    recv_sem=spec_recv,
                    device_id={"band": to},
                    device_id_type=MESH,
                ).start()

        @pl.when(my_block == k + PASS_DELAY)
        def _():
            wait_own()
            pass_on().start()

        return carry

    def wait_own():
        pltpu.make_async_copy(own.at[others], own.at[others], spec_recv).wait()

    def pass_on():
        return pltpu.make_async_remote_copy(
            src_ref=own,
            dst_ref=following,
            send_sem=pass_send,
            recv_sem=pass_recv,
            device_id={"band": lax.rem(me + n - 1, n)},
            device_id_type=MESH,
        )

    lax.fori_loop(0, BLOCKS, one_block, 0)

    @pl.when(my_block < PASS_DELAY)
    def _():
        wait_own()

    @pl.when((my_block != 0) & (my_block < PASS_DELAY))
    def _():
        pass_on().start()

    @pl.when(my_block != 0)
    def _():
        pass_on().wait_send()

    @pl.when(my_block == BLOCKS - 1)
    def _():
        following[...] = jnp.zeros_like(following)

    @pl.when(my_block != BLOCKS - 1)
    def _():
        pltpu.make_async_copy(following, following, pass_recv).wait()

    outs = [
        pltpu.make_async_copy(own, own_out, out_sem.at[0]),
        pltpu.make_async_copy(following, next_out, out_sem.at[1]),
    ]
    for copy in outs:
        copy.start()
    for copy in outs:
        copy.wait()

    def finish(k, carry):
        pltpu.make_async_copy(clean.at[k], cleaned.at[k], clean_sem.at[k]).wait()
        return carry

    lax.fori_loop(0, BLOCKS, finish, 0)
    sent = records.at[pl.ds(0, (n - 1) * BLOCKS * stripe)]
    pltpu.make_async_copy(sent, sent, raw_send).wait()
    pltpu.make_async_copy(infos.at[others], infos.at[others], info_send).wait()
    pltpu.make_async_copy(own.at[others], own.at[others], spec_send).wait()


def exchange(records, source, weight, gap_mask, n):
    channels, shard_len = records.shape
    stripe = channels // BLOCKS // n
    bands = n // BLOCKS
    span = n * shard_len
    hbm = pl.BlockSpec(memory_space=pl.ANY)
    gathered = jax.ShapeDtypeStruct((n, stripe, 2 * FB), jnp.bfloat16)
    dma = pltpu.SemaphoreType.DMA
    return pl.pallas_call(
        functools.partial(exchange_kernel, n),
        out_shape=(
            jax.ShapeDtypeStruct((BLOCKS, stripe, span), jnp.bfloat16),
            gathered,
            gathered,
        ),
        in_specs=[hbm, hbm, hbm, hbm],
        out_specs=(hbm, hbm, hbm),
        scratch_shapes=[
            pltpu.VMEM(records.shape, records.dtype),
            pltpu.VMEM((1, shard_len), jnp.int32),
            pltpu.VMEM((1, shard_len), jnp.float32),
            pltpu.VMEM((1, shard_len), jnp.int32),
            dma((3,)),
            dma((BLOCKS,)),
            pltpu.VMEM((2 * HALO, shard_len), jnp.float32),
            pltpu.VMEM((n, 2 * HALO, shard_len), jnp.float32),
            pltpu.VMEM((BLOCKS, n + 1, stripe, shard_len), jnp.bfloat16),
            pltpu.VMEM((n, stripe, shard_len), jnp.float32),
            pltpu.VMEM((BLOCKS, stripe, span), jnp.bfloat16),
            pltpu.VMEM((span, 2 * FB * bands), jnp.bfloat16),
            pltpu.VMEM((BLOCKS, bands, stripe, 2 * FB), jnp.bfloat16),
            pltpu.VMEM((n, stripe, 2 * FB), jnp.bfloat16),
            pltpu.VMEM((n, stripe, 2 * FB), jnp.bfloat16),
            dma,
            dma,
            dma,
            dma((BLOCKS,)),
            dma((BLOCKS,)),
            dma((BLOCKS,)),
            dma,
            dma,
            dma,
            dma,
            dma((2,)),
        ],
        compiler_params=pltpu.CompilerParams(
            collective_id=0, has_side_effects=True, vmem_limit_bytes=60 * 2**20
        ),
        name="exchange",
    )(records, source.reshape(1, -1), weight.reshape(1, -1), gap_mask.reshape(1, -1))


def tiles_kernel(own_in, next_in, cleaned, tiles, cleaned_out, raw, left, right, clean, made, sems):
    tile_sem, raw_sem, clean_sem = sems
    fetches = [
        pltpu.make_async_copy(block, raw.at[p], raw_sem.at[p])
        for p, block in enumerate((own_in, next_in))
    ]
    for copy in fetches:
        copy.start()
    clean_fetch = pltpu.make_async_copy(cleaned, clean, clean_sem.at[0])
    clean_store = pltpu.make_async_copy(clean, cleaned_out, clean_sem.at[1])
    clean_fetch.start()
    negate = lax.broadcasted_iota(jnp.int32, raw.shape[1:], 1) >= FB

    def store(p, part):
        t = 2 * p + part
        return pltpu.make_async_copy(made.at[t], tiles.at[0, p, part], tile_sem.at[t])

    for p in range(2):
        fetches[p].wait()
        values = raw[p].astype(jnp.float32)
        band_power = jnp.sum(values * values, axis=1, keepdims=True) / FB
        white = (values * lax.rsqrt(band_power + epsilon)).astype(jnp.bfloat16)
        if p == 0:
            left[...] = white
        right[0] = white
        turned = pltpu.roll(white.astype(jnp.float32), FB, 1)
        right[1] = jnp.where(negate, -turned, turned).astype(jnp.bfloat16)

        def make(part, carry):
            product = lax.dot_general(
                left[...],
                right[part],
                (((1,), (1,)), ((), ())),
                preferred_element_type=jnp.float32,
            )
            made[2 * p + part] = (product * (1.0 / FB)).astype(made.dtype)
            store(p, part).start()
            return carry

        lax.fori_loop(0, 2, make, 0)
        if p == 0:
            clean_fetch.wait()
            clean_store.start()
    for t in range(4):
        store(t // 2, t % 2).wait()
    clean_store.wait()


def make_tiles(own, following, cleaned):
    width = own.shape[0]
    hbm = pl.BlockSpec(memory_space=pl.ANY)
    dma = pltpu.SemaphoreType.DMA
    return pl.pallas_call(
        tiles_kernel,
        out_shape=(
            jax.ShapeDtypeStruct((1, 2, 2, width, width), jnp.bfloat16),
            jax.ShapeDtypeStruct(cleaned.shape, cleaned.dtype),
        ),
        in_specs=[hbm, hbm, hbm],
        out_specs=(hbm, hbm),
        scratch_shapes=[
            pltpu.VMEM((2, width, 2 * FB), jnp.bfloat16),
            pltpu.VMEM((width, 2 * FB), jnp.bfloat16),
            pltpu.VMEM((2, width, 2 * FB), jnp.bfloat16),
            pltpu.VMEM(cleaned.shape, cleaned.dtype),
            pltpu.VMEM((4, width, width), jnp.bfloat16),
            (dma((4,)), dma((2,)), dma((2,))),
        ],
        compiler_params=pltpu.CompilerParams(vmem_limit_bytes=60 * 2**20),
        name="tiles",
    )(own, following, cleaned)


def per_device(records, source, weight, gap_mask):
    n = lax.axis_size("band")
    channels, shard_len = records.shape
    stripe = channels // BLOCKS // n
    span = n * shard_len
    if stripe % 16 or shard_len != 128 or span & (span - 1) or span > 4096:
        return per_device_collectives(records, source, weight, gap_mask)
    cleaned, own, following = exchange(records, source, weight, gap_mask, n)
    width = n * stripe
    tiles, cleaned = make_tiles(own.reshape(width, -1), following.reshape(width, -1), cleaned)
    return cleaned, tiles


def solution(mesh):
    placed = (
        P(None, ("groups", "band")),
        P(("groups", "band")),
        P(("groups", "band")),
        P(("groups", "band")),
    )
    return jax.shard_map(
        per_device,
        mesh=mesh,
        in_specs=placed,
        out_specs=(P(None, "band", "groups"), P(("groups", "band"), None, None, None, None)),
        check_vma=False,
    )
```

```python
import functools
import math

import jax
import jax.numpy as jnp
from jax import lax
from jax.experimental import pallas as pl
from jax.experimental.pallas import tpu as pltpu
from jax.sharding import PartitionSpec as P

BLOCKS = 8
HALO = 8
FB = 64
F_LO = 16


epsilon = 1e-06


def passed_along(block, axis, distance):
    devices = range(lax.axis_size(axis))
    route = [(i - distance, i) for i in devices if i - distance in devices]
    return lax.ppermute(block, axis, route)


def harmonic_matrix(acquisition_moments, spectral_line_total, trace_duration):
    cycles_per_second = F_LO + jnp.arange(spectral_line_total, dtype=jnp.int32)
    angle_step = acquisition_moments[:, None] * cycles_per_second[None, :] % trace_duration
    phase_angle = angle_step.astype(jnp.float32) * (2.0 * math.pi / trace_duration)
    return jnp.concatenate([jnp.cos(phase_angle), -jnp.sin(phase_angle)], axis=1).astype(
        jnp.bfloat16
    )


def spread_matrix(source, weight, gap_mask, span):
    positions = jnp.arange(span, dtype=jnp.int32)[:, None]
    lower_hit = (positions == source[..., None, :]).astype(jnp.float32)
    upper_hit = (positions == source[..., None, :] + 1).astype(jnp.float32)
    mask_float = gap_mask.astype(jnp.float32)[..., None, :]
    return mask_float * (
        (1.0 - weight[..., None, :]) * lower_hit + weight[..., None, :] * upper_hit
    )


def whiten(spectra):
    values = spectra.astype(jnp.float32)
    band_power = jnp.sum(values * values, axis=(-3, -2)) / values.shape[-2]
    return (values * lax.rsqrt(band_power + epsilon)[..., None, None, :]).astype(jnp.bfloat16)


def pair_tiles(own_block, following):
    stacked_bins = own_block.shape[0] * own_block.shape[1]
    left_side = own_block.reshape(stacked_bins, -1).astype(jnp.float32)

    def columns(spectra):
        return jnp.stack(
            [spectra.reshape(stacked_bins, -1), jnp.concatenate([spectra[1], -spectra[0]], axis=0)]
        )

    right_side = jnp.concatenate([columns(own_block), columns(following)], axis=0).astype(
        jnp.float32
    )
    pair_tile = jnp.einsum("fi,pfj->pij", left_side, right_side, precision=lax.Precision.HIGHEST)
    width_out = left_side.shape[1]
    return (pair_tile / own_block.shape[1]).astype(jnp.bfloat16).reshape(2, 2, width_out, width_out)


def per_device_collectives(records, source, weight, gap_mask):
    devices = lax.axis_size("band")
    channels, shard_len = records.shape
    block_width = channels // BLOCKS
    mask_float = gap_mask.astype(jnp.float32)
    carried = passed_along(records[:, :HALO], "band", -1)
    padded = jnp.concatenate([records, carried], axis=1).astype(jnp.float32)
    spreader = spread_matrix(source, weight, gap_mask, shard_len + HALO)
    resampled = jnp.dot(padded, spreader, precision=lax.Precision.HIGHEST)
    totals, valid_count = lax.psum((jnp.sum(resampled, axis=1), jnp.sum(mask_float)), "band")
    local_clean = (mask_float * (resampled - (totals / valid_count)[:, None])).astype(jnp.bfloat16)
    cleaned = lax.all_to_all(
        local_clean.reshape(BLOCKS, block_width, shard_len),
        "band",
        split_axis=1,
        concat_axis=2,
        tiled=True,
    )
    taper_span = cleaned.shape[2]
    stripe_rows = cleaned.reshape(-1, taper_span)
    band_count = devices // BLOCKS
    spectral_line_total = FB * band_count
    segment_span = min(1024, taper_span)

    def accumulate(block_step, running):
        first_moment = block_step * segment_span
        window_rows = lax.dynamic_slice_in_dim(stripe_rows, first_moment, segment_span, 1).astype(
            jnp.float32
        )
        acquisition_moments = first_moment + jnp.arange(segment_span, dtype=jnp.int32)
        kernel_part = harmonic_matrix(acquisition_moments, spectral_line_total, taper_span).astype(
            jnp.float32
        )
        return running + jnp.dot(window_rows, kernel_part, precision=lax.Precision.HIGHEST)

    spectrum = lax.fori_loop(
        0,
        taper_span // segment_span,
        accumulate,
        jnp.zeros((stripe_rows.shape[0], 2 * spectral_line_total), jnp.float32),
    )
    spectrum = spectrum.astype(jnp.bfloat16)
    band_parts = spectrum.reshape(BLOCKS, -1, 2, band_count, FB).transpose(3, 0, 2, 4, 1)
    stripe_width = band_parts.shape[4]
    arrived = lax.all_to_all(
        band_parts.reshape(devices, 2, FB, stripe_width),
        "band",
        split_axis=0,
        concat_axis=3,
        tiled=True,
    )
    own_block = whiten(arrived[0])
    neighbour = passed_along(own_block, "band", -1)
    position = lax.axis_index("band") % BLOCKS
    following = jnp.where(position == BLOCKS - 1, jnp.zeros_like(neighbour), neighbour)
    return (cleaned, pair_tiles(own_block, following)[None])


LOOKAHEAD = 2
PASS_DELAY = 2
MESH = pl.DeviceIdType.MESH


def half_turn_cosine(steps, turn):
    folded = jnp.minimum(steps, turn - steps).astype(jnp.float32)
    y = (0.25 * turn - folded) * (2.0 * math.pi / turn)
    y2 = y * y
    total = jnp.full_like(y, -1.0 / 39916800.0)
    for term in (1.0 / 362880.0, -1.0 / 5040.0, 1.0 / 120.0, -1.0 / 6.0, 1.0):
        total = total * y2 + term
    return total * y


def exchange_kernel(
    n,
    records_in,
    source_in,
    weight_in,
    gap_mask_in,
    cleaned,
    own_out,
    next_out,
    records,
    source,
    weight,
    gap_mask,
    small_sem,
    fetch_sem,
    info,
    infos,
    raw,
    resampled,
    clean,
    table,
    spectra,
    own,
    following,
    info_send,
    info_recv,
    raw_send,
    raw_recv,
    raw_local,
    clean_sem,
    spec_send,
    spec_recv,
    pass_send,
    pass_recv,
    direct_send,
    direct_recv,
    out_sem,
):
    me = lax.axis_index("band")
    shard_len = records.shape[1]
    block_width = records.shape[0] // BLOCKS
    stripe = block_width // n
    bands = n // BLOCKS
    span = n * shard_len
    my_block = lax.rem(me, BLOCKS)
    last = BLOCKS - 1

    barrier = pltpu.get_barrier_semaphore()

    def greet(j, carry):
        pl.semaphore_signal(
            barrier, inc=1, device_id={"band": lax.rem(me + j, n)}, device_id_type=MESH
        )
        return carry

    lax.fori_loop(1, n, greet, 0)

    small = [
        pltpu.make_async_copy(there, here, small_sem.at[a])
        for a, (there, here) in enumerate(
            ((source_in, source), (weight_in, weight), (gap_mask_in, gap_mask))
        )
    ]
    for copy in small:
        copy.start()

    def fetch(k):
        rows = pl.ds(pl.multiple_of(k * block_width, block_width), block_width)
        return pltpu.make_async_copy(records_in.at[rows], records.at[rows], fetch_sem.at[k])

    for k in range(BLOCKS):
        fetch(k).start()
    for copy in small:
        copy.wait()

    row = lax.broadcasted_iota(jnp.int32, (HALO, shard_len), 0)
    lane = lax.broadcasted_iota(jnp.int32, (HALO, shard_len), 1)
    offset = source[...] - lane
    mask_row = gap_mask[...].astype(jnp.float32)
    upper = weight[...]
    info[:HALO] = mask_row * (
        jnp.where(offset == row, 1.0 - upper, 0.0) + jnp.where(offset + 1 == row, upper, 0.0)
    )
    info[HALO:] = jnp.broadcast_to(mask_row, (HALO, shard_len))
    infos[me] = info[...]

    def local_copy(k):
        start = pl.multiple_of(k * block_width + me * stripe, stripe)
        return pltpu.make_async_copy(
            records.at[pl.ds(start, stripe)], raw.at[k, me], raw_local.at[k]
        )

    pl.semaphore_wait(barrier, n - 1)

    def send_info(j, carry):
        pltpu.make_async_remote_copy(
            src_ref=info,
            dst_ref=infos.at[me],
            send_sem=info_send,
            recv_sem=info_recv,
            device_id={"band": lax.rem(me + j, n)},
            device_id_type=MESH,
        ).start()
        return carry


    def send_block(k):
        fetch(k).wait()
        local_copy(k).start()

        def send(j, carry):
            turn = (j % 2) * (n // 2) + j // 2
            to, bit = 0, 1
            while bit < n:
                to = to + bit * ((me // bit + turn // bit) % 2)
                bit *= 2
            start = pl.multiple_of(k * block_width + to * stripe, stripe)
            pltpu.make_async_remote_copy(
                src_ref=records.at[pl.ds(start, stripe)],
                dst_ref=raw.at[k, me],
                send_sem=raw_send,
                recv_sem=raw_recv.at[k],
                device_id={"band": to},
                device_id_type=MESH,
            ).start()
            return carry

        lax.fori_loop(1, n, send, 0)

    send_block(0)
    lax.fori_loop(1, n, send_info, 0)
    for k in range(1, LOOKAHEAD):
        send_block(k)

    for k in range(BLOCKS):
        raw[k, n] = jnp.zeros((stripe, shard_len), raw.dtype)

    moments = 128

    def fill(step, carry):
        shape = (moments, 2 * FB)
        t = step * moments + lax.broadcasted_iota(jnp.int32, shape, 0)
        column = lax.broadcasted_iota(jnp.int32, shape, 1)
        part = column // FB
        for q in range(bands):
            f = F_LO + q * FB + column - part * FB
            steps = (t * f + part * (span // 4)) & (span - 1)
            start = pl.multiple_of(step * moments, moments)
            table[pl.ds(start, moments), q * 2 * FB : (q + 1) * 2 * FB] = half_turn_cosine(
                steps, span
            ).astype(table.dtype)
        return carry

    lax.fori_loop(0, span // moments, fill, 0)

    others = pl.ds(0, n - 1)
    pltpu.make_async_copy(infos.at[others], infos.at[others], info_recv).wait()
    count = jnp.sum(infos[:, HALO, :])

    lane = lax.broadcasted_iota(jnp.int32, (stripe, shard_len), 1)

    def one_block(k, carry):
        @pl.when(k + LOOKAHEAD < BLOCKS)
        def _():
            send_block(k + LOOKAHEAD)

        pltpu.make_async_copy(raw.at[k, others], raw.at[k, others], raw_recv.at[k]).wait()
        local_copy(k).wait()

        def resample_one(s, total):
            here = raw[k, s].astype(jnp.float32)
            after = raw[k, s + 1].astype(jnp.float32)
            value = here * infos[s, 0:1, :]
            for d in range(1, HALO):
                shifted = pltpu.roll(jnp.where(lane >= d, here, after), shard_len - d, 1)
                value = value + shifted * infos[s, d : d + 1, :]
            resampled[s] = value
            return total + value

        def resample(group, total):
            for s in range(4):
                total = resample_one(4 * group + s, total)
            return total

        total = lax.fori_loop(0, n // 4, resample, jnp.zeros((stripe, shard_len), jnp.float32))
        centre = jnp.sum(total, axis=1, keepdims=True) / count
        for s in range(n):
            clean[k, :, s * shard_len : (s + 1) * shard_len] = (
                infos[s, HALO : HALO + 1, :] * (resampled[s] - centre)
            ).astype(clean.dtype)
        pltpu.make_async_copy(clean.at[k], cleaned.at[k], clean_sem.at[k]).start()
        result = jnp.dot(clean[k], table[...], preferred_element_type=jnp.float32)
        for q in range(bands):
            spectra[k, q] = result[:, q * 2 * FB : (q + 1) * 2 * FB].astype(spectra.dtype)
            to = q * BLOCKS + k

            @pl.when(to == me)
            def _():
                own[me] = spectra[k, q]

            @pl.when(to != me)
            def _():
                pltpu.make_async_remote_copy(
                    src_ref=spectra.at[k, q],
                    dst_ref=own.at[me],
                    send_sem=spec_send,
                    recv_sem=spec_recv,
                    device_id={"band": to},
                    device_id_type=MESH,
                ).start()

        @pl.when((my_block == k - PASS_DELAY) & (my_block > 0))
        def _():
            wait_own()
            pass_on().start()

        return carry

    def wait_own():
        pltpu.make_async_copy(own.at[others], own.at[others], spec_recv).wait()

    def pass_on():
        return pltpu.make_async_remote_copy(
            src_ref=own,
            dst_ref=following,
            send_sem=pass_send,
            recv_sem=pass_recv,
            device_id={"band": lax.rem(me + n - 1, n)},
            device_id_type=MESH,
        )

    def direct(q):
        return pltpu.make_async_remote_copy(
            src_ref=spectra.at[last, q],
            dst_ref=following.at[me],
            send_sem=direct_send.at[q],
            recv_sem=direct_recv,
            device_id={"band": q * BLOCKS + last - 1},
            device_id_type=MESH,
        )

    lax.fori_loop(0, BLOCKS, one_block, 0)

    for q in range(bands):

        @pl.when(me != q * BLOCKS + last - 1)
        def _():
            direct(q).start()

        @pl.when(me == q * BLOCKS + last - 1)
        def _():
            following[me] = spectra[last, q]

    @pl.when((my_block == 0) | (my_block > last - PASS_DELAY))
    def _():
        wait_own()

    @pl.when((my_block > last - PASS_DELAY) & (my_block < last))
    def _():
        pass_on().start()

    @pl.when((my_block > 0) & (my_block < last))
    def _():
        pass_on().wait_send()

    @pl.when(my_block == last)
    def _():
        following[...] = jnp.zeros_like(following)

    @pl.when(my_block == last - 1)
    def _():
        pltpu.make_async_copy(following.at[others], following.at[others], direct_recv).wait()

    @pl.when(my_block < last - 1)
    def _():
        pltpu.make_async_copy(following, following, pass_recv).wait()

    for q in range(bands):

        @pl.when(me != q * BLOCKS + last - 1)
        def _():
            direct(q).wait_send()

    outs = [
        pltpu.make_async_copy(own, own_out, out_sem.at[0]),
        pltpu.make_async_copy(following, next_out, out_sem.at[1]),
    ]
    for copy in outs:
        copy.start()
    for copy in outs:
        copy.wait()

    def finish(k, carry):
        pltpu.make_async_copy(clean.at[k], cleaned.at[k], clean_sem.at[k]).wait()
        return carry

    lax.fori_loop(0, BLOCKS, finish, 0)
    sent = records.at[pl.ds(0, (n - 1) * BLOCKS * stripe)]
    pltpu.make_async_copy(sent, sent, raw_send).wait()
    pltpu.make_async_copy(infos.at[others], infos.at[others], info_send).wait()
    pltpu.make_async_copy(own.at[others], own.at[others], spec_send).wait()


def exchange(records, source, weight, gap_mask, n):
    channels, shard_len = records.shape
    stripe = channels // BLOCKS // n
    bands = n // BLOCKS
    span = n * shard_len
    hbm = pl.BlockSpec(memory_space=pl.ANY)
    gathered = jax.ShapeDtypeStruct((n, stripe, 2 * FB), jnp.bfloat16)
    dma = pltpu.SemaphoreType.DMA
    return pl.pallas_call(
        functools.partial(exchange_kernel, n),
        out_shape=(
            jax.ShapeDtypeStruct((BLOCKS, stripe, span), jnp.bfloat16),
            gathered,
            gathered,
        ),
        in_specs=[hbm, hbm, hbm, hbm],
        out_specs=(hbm, hbm, hbm),
        scratch_shapes=[
            pltpu.VMEM(records.shape, records.dtype),
            pltpu.VMEM((1, shard_len), jnp.int32),
            pltpu.VMEM((1, shard_len), jnp.float32),
            pltpu.VMEM((1, shard_len), jnp.int32),
            dma((3,)),
            dma((BLOCKS,)),
            pltpu.VMEM((2 * HALO, shard_len), jnp.float32),
            pltpu.VMEM((n, 2 * HALO, shard_len), jnp.float32),
            pltpu.VMEM((BLOCKS, n + 1, stripe, shard_len), jnp.bfloat16),
            pltpu.VMEM((n, stripe, shard_len), jnp.float32),
            pltpu.VMEM((BLOCKS, stripe, span), jnp.bfloat16),
            pltpu.VMEM((span, 2 * FB * bands), jnp.bfloat16),
            pltpu.VMEM((BLOCKS, bands, stripe, 2 * FB), jnp.bfloat16),
            pltpu.VMEM((n, stripe, 2 * FB), jnp.bfloat16),
            pltpu.VMEM((n, stripe, 2 * FB), jnp.bfloat16),
            dma,
            dma,
            dma,
            dma((BLOCKS,)),
            dma((BLOCKS,)),
            dma((BLOCKS,)),
            dma,
            dma,
            dma,
            dma,
            dma((bands,)),
            dma,
            dma((2,)),
        ],
        compiler_params=pltpu.CompilerParams(
            collective_id=0, has_side_effects=True, vmem_limit_bytes=60 * 2**20
        ),
        name="exchange",
    )(records, source.reshape(1, -1), weight.reshape(1, -1), gap_mask.reshape(1, -1))


def tiles_kernel(own_in, next_in, cleaned, tiles, cleaned_out, raw, left, right, clean, made, sems):
    tile_sem, raw_sem, clean_sem = sems
    fetches = [
        pltpu.make_async_copy(block, raw.at[p], raw_sem.at[p])
        for p, block in enumerate((own_in, next_in))
    ]
    for copy in fetches:
        copy.start()
    clean_fetch = pltpu.make_async_copy(cleaned, clean, clean_sem.at[0])
    clean_store = pltpu.make_async_copy(clean, cleaned_out, clean_sem.at[1])
    clean_fetch.start()
    negate = lax.broadcasted_iota(jnp.int32, raw.shape[1:], 1) >= FB

    def store(p, part):
        t = 2 * p + part
        return pltpu.make_async_copy(made.at[t], tiles.at[0, p, part], tile_sem.at[t])

    for p in range(2):
        fetches[p].wait()
        values = raw[p].astype(jnp.float32)
        band_power = jnp.sum(values * values, axis=1, keepdims=True) / FB
        white = (values * lax.rsqrt(band_power + epsilon)).astype(jnp.bfloat16)
        if p == 0:
            left[...] = white
        right[0] = white
        turned = pltpu.roll(white.astype(jnp.float32), FB, 1)
        right[1] = jnp.where(negate, -turned, turned).astype(jnp.bfloat16)

        def make(part, carry):
            product = lax.dot_general(
                left[...],
                right[part],
                (((1,), (1,)), ((), ())),
                preferred_element_type=jnp.float32,
            )
            made[2 * p + part] = (product * (1.0 / FB)).astype(made.dtype)
            store(p, part).start()
            return carry

        lax.fori_loop(0, 2, make, 0)
        if p == 0:
            clean_fetch.wait()
            clean_store.start()
    for t in range(4):
        store(t // 2, t % 2).wait()
    clean_store.wait()


def make_tiles(own, following, cleaned):
    width = own.shape[0]
    hbm = pl.BlockSpec(memory_space=pl.ANY)
    dma = pltpu.SemaphoreType.DMA
    return pl.pallas_call(
        tiles_kernel,
        out_shape=(
            jax.ShapeDtypeStruct((1, 2, 2, width, width), jnp.bfloat16),
            jax.ShapeDtypeStruct(cleaned.shape, cleaned.dtype),
        ),
        in_specs=[hbm, hbm, hbm],
        out_specs=(hbm, hbm),
        scratch_shapes=[
            pltpu.VMEM((2, width, 2 * FB), jnp.bfloat16),
            pltpu.VMEM((width, 2 * FB), jnp.bfloat16),
            pltpu.VMEM((2, width, 2 * FB), jnp.bfloat16),
            pltpu.VMEM(cleaned.shape, cleaned.dtype),
            pltpu.VMEM((4, width, width), jnp.bfloat16),
            (dma((4,)), dma((2,)), dma((2,))),
        ],
        compiler_params=pltpu.CompilerParams(vmem_limit_bytes=60 * 2**20),
        name="tiles",
    )(own, following, cleaned)


def per_device(records, source, weight, gap_mask):
    n = lax.axis_size("band")
    channels, shard_len = records.shape
    stripe = channels // BLOCKS // n
    span = n * shard_len
    if stripe % 16 or shard_len != 128 or span & (span - 1) or span > 4096:
        return per_device_collectives(records, source, weight, gap_mask)
    cleaned, own, following = exchange(records, source, weight, gap_mask, n)
    width = n * stripe
    tiles, cleaned = make_tiles(own.reshape(width, -1), following.reshape(width, -1), cleaned)
    return cleaned, tiles


def solution(mesh):
    placed = (
        P(None, ("groups", "band")),
        P(("groups", "band")),
        P(("groups", "band")),
        P(("groups", "band")),
    )
    return jax.shard_map(
        per_device,
        mesh=mesh,
        in_specs=placed,
        out_specs=(P(None, "band", "groups"), P(("groups", "band"), None, None, None, None)),
        check_vma=False,
    )
```
